32 devices in a mesh: gx: 8 (over y, x, core), gy: 4 (over z).
Axes of the slice: x: 2, y: 2, z: 4, core: 2. Of those that a mesh axis runs over, the one named last changes fastest.
Arguments:
- right_sides: bfloat16 [8, 4, 320, 1024], P('gx', 'gy'), may hold values from -2.5 to 2.5
- old_state: bfloat16 [8, 4, 320, 1024], P('gx', 'gy'), may hold values from -2.5 to 2.5
- plane_coupling: bfloat16 [8, 4, 2, 320, 320], P('gx', 'gy'), may hold values from -1.25 to 1.25
- face_coupling: bfloat16 [8, 4, 4, 320, 320], P('gx', 'gy'), may hold values from -0.25 to 0.25
- diag_inverse: bfloat16 [8, 4, 320, 320], P('gx', 'gy'), may hold values from -2 to 2
- neighbours: int32 [8, 4, 4], P('gx', 'gy'), may hold values from 0 to 2, as said below
Outputs:
- final_state: bfloat16 [8, 4, 320, 1024], P('gx', 'gy')
The draws below stay inside these ranges and needn't reach their ends.
Inputs may be any that keep to these rules, and one draw needn't show every extreme that they name: `neighbours`: face 0 names one of the previous strip's elements (0 to 0), face 1 one of the next strip's (2 to 2); faces 2 and 3 may name any of the 3 candidates.
All inputs are finite; a program needn't handle non-finite values.
Results may differ from the reference program's by a relative error of at most 0.035.
Values may be sent and summed in bfloat16 or wider, within the bound.
A program may use at most 64 MiB of HBM per device.

```python
import jax
import jax.numpy as jnp
from jax import lax

B = 320
E_DEV = 1
RHS = 1024
PLANES = 8
ELEMENTS = 4


def draw_plane_coupling(key, part):
    noise_key = jax.random.fold_in(key, 37)
    full_shape = (PLANES, ELEMENTS, 2, B, B)
    noise = jnp.clip(jax.random.normal(noise_key, full_shape, jnp.float32), -4.5, 4.5)
    strength = 1.46
    values = strength * noise / jnp.sqrt(B * 1.0)
    return values.astype(jnp.bfloat16)


def draw_diag_inverse(key, part):
    noise_key = jax.random.fold_in(jax.random.fold_in(key, 11), 0)
    identity = jnp.eye(B, dtype=jnp.float32)
    full_shape = (PLANES, ELEMENTS, B, B)
    noise = jax.random.normal(noise_key, full_shape, jnp.float32)
    row_scale = jnp.ones((PLANES, ELEMENTS, B, 1), jnp.float32)
    values = 0.6 * (identity * row_scale + 0.35 * noise / jnp.sqrt(B * 1.0))
    return values.astype(jnp.bfloat16)


def draw_neighbours(key, part):
    first_key, second_key, other_key = jax.random.split(jax.random.fold_in(key, 23), 3)
    draw_shape = (PLANES, ELEMENTS, 1)
    below_side = jax.random.randint(first_key, draw_shape, 0, E_DEV)
    above_side = jax.random.randint(second_key, draw_shape, 2 * E_DEV, 3 * E_DEV)
    others = jax.random.randint(other_key, (PLANES, ELEMENTS, 2), 0, 3 * E_DEV)
    return jnp.concatenate([below_side, above_side, others], axis=2).astype(jnp.int32)


def shard_levels(key, dims, cuts, smallest, largest):
    loudness = 1.0
    for position, blocks in cuts:
        steps = jax.random.uniform(jax.random.fold_in(jax.random.fold_in(key, 6), position), (blocks,), jnp.float32, smallest / len(cuts), largest / len(cuts))
        loudness = loudness * jnp.repeat(jnp.exp(steps), dims[position] // blocks).reshape((-1,) + (1,) * (len(dims) - 1 - position))
    return loudness


def centred(own_key, shape, scale, reach, shards=(), held_as=jnp.bfloat16):
    array = scale * jax.random.normal(own_key, shape, jnp.float32)
    if shards:
        array = array * shard_levels(own_key, shape, shards, -0.22, 0.18)
    return jnp.clip(array, -reach, reach).astype(held_as)


def setup_inputs(seed: int = 0) -> dict:
    seeds = jax.random.split(jax.random.key(seed), 7)
    right_sides = centred(seeds[0], (PLANES, ELEMENTS, B, RHS), 0.2, 2.5, ((0, 8), (1, 4)))
    old_state = centred(seeds[1], (PLANES, ELEMENTS, B, RHS), 0.2, 2.5, ((0, 8), (1, 4)))
    plane_coupling = draw_plane_coupling(jax.random.fold_in(seeds[6], 71), 0)
    face_coupling = centred(seeds[3], (PLANES, ELEMENTS, 4, B, B), (2 * B) ** -0.5, 0.25, ((0, 8), (1, 4)))
    diag_inverse = draw_diag_inverse(jax.random.fold_in(seeds[6], 71), 0)
    neighbours = draw_neighbours(jax.random.fold_in(seeds[6], 71), 0)
    return {"right_sides": right_sides, "old_state": old_state, "plane_coupling": plane_coupling, "face_coupling": face_coupling, "diag_inverse": diag_inverse, "neighbours": neighbours}


def apply_block(blocks, states):
    return jnp.einsum("gij,gjr->gir", blocks.astype(jnp.float32), states.astype(jnp.float32))


def in_plane(states, link_table, face_blocks):
    padded = jnp.pad(states, ((E_DEV, E_DEV), (0, 0), (0, 0)))
    anchor = (jnp.arange(states.shape[0], dtype=jnp.int32) // E_DEV) * E_DEV
    index_rows = (anchor[:, None] + link_table).astype(jnp.int32)
    picked = padded[index_rows]
    return jnp.einsum("gfij,gfjr->gir", face_blocks.astype(jnp.float32), picked.astype(jnp.float32))


def reference(right_sides, old_state, plane_coupling, face_coupling, diag_inverse, neighbours):
    old_after = jnp.concatenate([old_state[1:], jnp.zeros_like(old_state[:1])], axis=0)
    initial = jnp.zeros(old_state.shape[1:], jnp.bfloat16)

    def forward_plane(previous, inputs):
        rhs_plane, old_here, old_next, coupling, face_blocks, inverse, link_table = inputs
        partial_sum = rhs_plane.astype(jnp.float32) - apply_block(coupling[:, 1], old_next)
        partial_sum = partial_sum - in_plane(old_here, link_table, face_blocks)
        lower_terms = apply_block(coupling[:, 0], previous)
        residual = (partial_sum - lower_terms).astype(jnp.bfloat16)
        half_here = apply_block(inverse, residual).astype(jnp.bfloat16)
        return half_here, half_here

    unused, half_state = lax.scan(forward_plane, initial, (right_sides, old_state, old_after, plane_coupling, face_coupling, diag_inverse, neighbours))
    half_before = jnp.concatenate([jnp.zeros_like(half_state[:1]), half_state[:-1]], axis=0)

    def backward_plane(following, inputs):
        rhs_plane, half_here, half_prior, coupling, face_blocks, inverse, link_table = inputs
        lower_terms = apply_block(coupling[:, 0], half_prior)
        partial_sum = rhs_plane.astype(jnp.float32) - lower_terms - in_plane(half_here, link_table, face_blocks)
        residual = (partial_sum - apply_block(coupling[:, 1], following)).astype(jnp.bfloat16)
        final_here = apply_block(inverse, residual).astype(jnp.bfloat16)
        return final_here, final_here

    unused, final_state = lax.scan(backward_plane, initial, (right_sides, half_state, half_before, plane_coupling, face_coupling, diag_inverse, neighbours), reverse=True)
    return final_state
```

```python
import functools

import jax
import jax.numpy as jnp
from jax import lax
from jax.experimental import pallas as pl
from jax.experimental.pallas import tpu as pltpu
from jax.sharding import PartitionSpec as P

PANELS = 4
LAG_FORWARD = (1, 1)
LAG_HALO = 1
LAG_BACKWARD = (1, 2)


def dot(a, b):
    return jnp.dot(a, b, preferred_element_type=jnp.float32)


def kernel(
    planes, strips, panels,
    right_hbm, old_hbm, plane_hbm, face_hbm, inverse_hbm, links,
    out_hbm,
    right, plane, face, inverse,
    old_stack, half_stack, old_weights, half_weights,
    lower_step, upper_step, own_step, pair_step, chip_step,
    base, rest, share, pair_share, half_in, final_in, final_out,
    load_sem, own_sem, store_sem,
    old_send, old_recv, halo_send, halo_recv,
    step_send, step_recv, share_send, share_recv,
    chain_send, relay_send, half_recv, final_recv,
):
    p, g = lax.axis_index("gx"), lax.axis_index("gy")
    size = inverse.shape[0]
    width = final_out.shape[2]
    odd = lax.rem(p, 2)
    even = odd == 0
    partner = p + 1 - 2 * odd
    chip, chips = p // 2, planes // 2
    has_prev, has_next = p >= 2, p < planes - 2
    below, above = g > 0, g < strips - 1

    def remote(src, dst, send, recv, plane_to, strip_to):
        return pltpu.make_async_remote_copy(
            src_ref=src, dst_ref=dst, send_sem=send, recv_sem=recv,
            device_id=(plane_to, strip_to), device_id_type=pl.DeviceIdType.MESH,
        )

    def columns(k):
        return pl.ds(pl.multiple_of(k * width, width), width)

    def rows(n):
        return pl.ds(n * size, size)

    def each(body):
        lax.fori_loop(0, panels, lambda k, c: (body(k), c)[1], 0)

    def old_panel(k):
        return old_hbm.at[0, 0, :, columns(k)]

    def old_up(k):
        return remote(old_panel(k), old_stack.at[k, rows(1)], old_send.at[k, 0], old_recv.at[k, 0], p, g + 1)

    def old_down(k):
        return remote(old_panel(k), old_stack.at[k, rows(3)], old_send.at[k, 1], old_recv.at[k, 1], p, g - 1)

    def old_back(k):
        return remote(old_panel(k), old_stack.at[k, rows(0)], old_send.at[k, 2], old_recv.at[k, 2], p - 1, g)

    def old_own(k):
        return pltpu.make_async_copy(old_panel(k), old_stack.at[k, rows(2)], own_sem.at[k])

    def halo_up(k):
        return remote(half_stack.at[k, rows(1)], half_stack.at[k, rows(0)], halo_send.at[k, 0], halo_recv.at[k, 0], p, g + 1)

    def halo_down(k):
        return remote(half_stack.at[k, rows(1)], half_stack.at[k, rows(2)], halo_send.at[k, 1], halo_recv.at[k, 1], p, g - 1)

    def step_copy():
        return remote(own_step, pair_step, step_send, step_recv, partner, g)

    def share_copy(k):
        return remote(share.at[k], pair_share.at[k], share_send.at[k], share_recv.at[k], partner, g)

    def half_chain(k):
        return remote(half_stack.at[k, rows(1)], half_in.at[k], chain_send.at[k], half_recv.at[k], p + 2, g)

    def half_relay(k):
        return remote(half_in.at[k], half_in.at[k], relay_send.at[k], half_recv.at[k], partner, g)

    def final_chain(k):
        return remote(final_out.at[k], final_in.at[k], chain_send.at[k], final_recv.at[k], p - 2, g)

    def final_relay(k):
        return remote(final_in.at[k], final_in.at[k], relay_send.at[k], final_recv.at[k], partner, g)

    def store(k):
        return pltpu.make_async_copy(final_out.at[k], out_hbm.at[0, 0, :, columns(k)], store_sem.at[k])

    loads = [
        pltpu.make_async_copy(plane_hbm.at[0, 0], plane, load_sem.at[0]),
        pltpu.make_async_copy(inverse_hbm.at[0, 0], inverse, load_sem.at[1]),
        pltpu.make_async_copy(face_hbm.at[0, 0], face, load_sem.at[2]),
        pltpu.make_async_copy(right_hbm.at[0, 0], right, load_sem.at[3]),
    ]

    barrier = pltpu.get_barrier_semaphore()
    greeted = (
        (below, p, g - 1), (above, p, g + 1), (p > 0, p - 1, g), (p < planes - 1, p + 1, g),
        (has_prev, p - 2, g), (has_next, p + 2, g),
    )
    for there, plane_to, strip_to in greeted:
        @pl.when(there)
        def _():
            pl.semaphore_signal(barrier, inc=1, device_id=(plane_to, strip_to), device_id_type=pl.DeviceIdType.MESH)
    for copy in loads:
        copy.start()
    each(lambda k: old_own(k).start())
    pl.semaphore_wait(barrier, sum(there.astype(jnp.int32) for there, _, _ in greeted))

    def send_old(k):
        pl.when(above)(lambda: old_up(k).start())
        pl.when(below)(lambda: old_down(k).start())
        pl.when(p > 0)(lambda: old_back(k).start())

    each(send_old)

    nothing = jnp.zeros((panels, size, width), jnp.bfloat16)

    @pl.when(jnp.logical_not(below))
    def _():
        old_stack[:, rows(1)] = nothing
        half_stack[:, rows(0)] = nothing

    @pl.when(jnp.logical_not(above))
    def _():
        old_stack[:, rows(3)] = nothing
        half_stack[:, rows(2)] = nothing

    @pl.when(p == planes - 1)
    def _():
        old_stack[:, rows(0)] = nothing

    @pl.when(jnp.logical_not(has_prev))
    def _():
        half_in[...] = nothing

    @pl.when(jnp.logical_not(has_next))
    def _():
        final_in[...] = nothing

    loads[0].wait()
    loads[1].wait()
    lower_step[...] = dot(inverse[...], plane[0]).astype(jnp.bfloat16)
    upper_step[...] = dot(inverse[...], plane[1]).astype(jnp.bfloat16)

    @pl.when(even)
    def _():
        own_step[...] = lower_step[...]

    @pl.when(odd == 1)
    def _():
        own_step[...] = upper_step[...]

    step_copy().start()
    loads[2].wait()
    old_weights[:, 0:size] = plane[1]
    for candidate in range(3):
        total = face[0 if candidate == 0 else 1].astype(jnp.float32) if candidate != 1 else None
        for f in (2, 3):
            named = jnp.where(links[0, 0, f] == candidate, 1.0, 0.0)
            term = face[f].astype(jnp.float32) * named
            total = term if total is None else total + term
        total = total.astype(jnp.bfloat16)
        old_weights[:, (candidate + 1) * size : (candidate + 2) * size] = total
        half_weights[:, candidate * size : (candidate + 1) * size] = total
    loads[3].wait()
    step_copy().wait()

    @pl.when(even)
    def _():
        chip_step[...] = dot(upper_step[...], pair_step[...]).astype(jnp.bfloat16)

    @pl.when(odd == 1)
    def _():
        chip_step[...] = dot(lower_step[...], pair_step[...]).astype(jnp.bfloat16)

    def prepare(k):
        old_own(k).wait()
        pl.when(p < planes - 1)(lambda: old_back(k).wait_recv())
        pl.when(below)(lambda: old_up(k).wait_recv())
        pl.when(above)(lambda: old_down(k).wait_recv())
        old_sum = right[:, columns(k)].astype(jnp.float32) - dot(old_weights[...], old_stack[k])
        value = dot(inverse[...], old_sum.astype(jnp.bfloat16))
        base[k] = value

        @pl.when(even)
        def _():
            share[k] = value.astype(jnp.bfloat16)
            share_copy(k).start()

    def send_half(k):
        pl.when(above)(lambda: halo_up(k).start())
        pl.when(below)(lambda: halo_down(k).start())

    def forward(k):
        @pl.when(odd == 1)
        def _():
            share_copy(k).wait_recv()
            before = pair_share[k]
            value = base[k] - dot(lower_step[...], before)

            @pl.when(has_prev)
            def _():
                half_chain(k).wait_recv()
                half_relay(k).start()

            arrived = half_in[k]
            half_stack[k, rows(1)] = (value + dot(chip_step[...], arrived)).astype(jnp.bfloat16)
            pl.when(has_next)(lambda: half_chain(k).start())
            send_half(k)
            prior = (before.astype(jnp.float32) - dot(pair_step[...], arrived)).astype(jnp.bfloat16)
            rest[k] = right[:, columns(k)].astype(jnp.float32) - dot(plane[0], prior)

        @pl.when(even)
        def _():
            pl.when(has_prev)(lambda: half_relay(k).wait_recv())
            arrived = half_in[k]
            half_stack[k, rows(1)] = (base[k] - dot(lower_step[...], arrived)).astype(jnp.bfloat16)
            send_half(k)
            rest[k] = right[:, columns(k)].astype(jnp.float32) - dot(plane[0], arrived)

    def turn_round(k):
        pl.when(below)(lambda: halo_up(k).wait_recv())
        pl.when(above)(lambda: halo_down(k).wait_recv())
        half_sum = rest[k] - dot(half_weights[...], half_stack[k])
        value = dot(inverse[...], half_sum.astype(jnp.bfloat16))
        base[k] = value

        @pl.when(odd == 1)
        def _():
            share[k] = value.astype(jnp.bfloat16)
            share_copy(k).start()

    def backward(k):
        @pl.when(even)
        def _():
            share_copy(k).wait_recv()
            value = base[k] - dot(upper_step[...], pair_share[k])

            @pl.when(has_next)
            def _():
                final_chain(k).wait_recv()
                final_relay(k).start()

            final_out[k] = (value + dot(chip_step[...], final_in[k])).astype(jnp.bfloat16)
            pl.when(has_prev)(lambda: final_chain(k).start())

        @pl.when(odd == 1)
        def _():
            pl.when(has_next)(lambda: final_relay(k).wait_recv())
            final_out[k] = (base[k] - dot(upper_step[...], final_in[k])).astype(jnp.bfloat16)

        store(k).start()

    to_forward = jnp.minimum(panels, LAG_FORWARD[0] + LAG_FORWARD[1] * chip)
    to_turn = to_forward + LAG_HALO
    to_backward = to_turn + jnp.minimum(panels, LAG_BACKWARD[0] + LAG_BACKWARD[1] * (chips - 1 - chip))

    def turn(t, carry):
        pl.when(t < panels)(lambda: prepare(t))
        for lag, stage in ((to_forward, forward), (to_turn, turn_round), (to_backward, backward)):
            k = t - lag
            pl.when((k >= 0) & (k < panels))(functools.partial(stage, k))
        return carry

    lax.fori_loop(0, panels + to_backward, turn, 0)

    def finish(k):
        store(k).wait()
        share_copy(k).wait_send()

        @pl.when(above)
        def _():
            old_up(k).wait_send()
            halo_up(k).wait_send()

        @pl.when(below)
        def _():
            old_down(k).wait_send()
            halo_down(k).wait_send()

        pl.when(p > 0)(lambda: old_back(k).wait_send())

        @pl.when(odd == 1)
        def _():
            pl.when(has_next)(lambda: half_chain(k).wait_send())
            pl.when(has_prev)(lambda: half_relay(k).wait_send())

        @pl.when(even)
        def _():
            pl.when(has_prev)(lambda: final_chain(k).wait_send())
            pl.when(has_next)(lambda: final_relay(k).wait_send())

    each(finish)


def local(planes, strips, right_sides, old_state, plane_coupling, face_coupling, diag_inverse, neighbours):
    size, total = right_sides.shape[2:]
    n = PANELS
    width = total // n
    half = functools.partial(pltpu.VMEM, dtype=jnp.bfloat16)
    single = functools.partial(pltpu.VMEM, dtype=jnp.float32)
    dma = pltpu.SemaphoreType.DMA
    anywhere = pl.BlockSpec(memory_space=pl.ANY)
    return pl.pallas_call(
        functools.partial(kernel, planes, strips, n),
        out_shape=jax.ShapeDtypeStruct(right_sides.shape, jnp.bfloat16),
        in_specs=[anywhere] * 5 + [pl.BlockSpec(memory_space=pltpu.SMEM)],
        out_specs=anywhere,
        scratch_shapes=[
            half((size, total)), half((2, size, size)), half((4, size, size)), half((size, size)),
            half((n, 4 * size, width)), half((n, 3 * size, width)), half((size, 4 * size)), half((size, 3 * size)),
            half((size, size)), half((size, size)), half((size, size)), half((size, size)), half((size, size)),
            single((n, size, width)), single((n, size, width)), half((n, size, width)), half((n, size, width)),
            half((n, size, width)), half((n, size, width)), half((n, size, width)),
            dma((4,)), dma((n,)), dma((n,)),
            dma((n, 3)), dma((n, 3)), dma((n, 2)), dma((n, 2)),
            dma, dma, dma((n,)), dma((n,)),
            dma((n,)), dma((n,)), dma((n,)), dma((n,)),
        ],
        compiler_params=pltpu.CompilerParams(
            collective_id=0, has_side_effects=True, vmem_limit_bytes=48 * 2**20
        ),
    )(right_sides, old_state, plane_coupling, face_coupling, diag_inverse, neighbours)


def solution(mesh):
    specs = [P("gx", "gy", *[None] * n) for n in (2, 2, 3, 3, 2, 1)]
    run = functools.partial(local, mesh.shape["gx"], mesh.shape["gy"])
    return jax.shard_map(run, mesh=mesh, in_specs=tuple(specs), out_specs=specs[0], check_vma=False)
```

```python
import functools

import jax
import jax.numpy as jnp
from jax import lax
from jax.experimental import pallas as pl
from jax.experimental.pallas import tpu as pltpu
from jax.sharding import PartitionSpec as P

PANELS = 8
LAG_FORWARD = (2, 2)
LAG_HALO = 3
LAG_BACKWARD = (3, 6)


def dot(a, b):
    return jnp.dot(a, b, preferred_element_type=jnp.float32)


def kernel(
    planes, strips, panels,
    right_hbm, old_hbm, plane_hbm, face_hbm, inverse_hbm, links,
    out_hbm,
    right, plane, face, inverse,
    old_stack, half_stack, old_weights, half_weights,
    lower_step, upper_step, own_step, pair_step, chip_step,
    base, rest, share, pair_share, half_in, final_in, final_out,
    load_sem, own_sem, store_sem,
    old_send, old_recv, halo_send, halo_recv,
    step_send, step_recv, share_send, share_recv,
    chain_send, relay_send, half_recv, final_recv,
):
    p, g = lax.axis_index("gx"), lax.axis_index("gy")
    size = inverse.shape[0]
    width = final_out.shape[2]
    odd = lax.rem(p, 2)
    even = odd == 0
    partner = p + 1 - 2 * odd
    chip, chips = p // 2, planes // 2
    has_prev, has_next = p >= 2, p < planes - 2
    below, above = g > 0, g < strips - 1

    def remote(src, dst, send, recv, plane_to, strip_to):
        return pltpu.make_async_remote_copy(
            src_ref=src, dst_ref=dst, send_sem=send, recv_sem=recv,
            device_id=(plane_to, strip_to), device_id_type=pl.DeviceIdType.MESH,
        )

    def columns(k):
        return pl.ds(pl.multiple_of(k * width, width), width)

    def rows(n):
        return pl.ds(n * size, size)

    def each(body):
        lax.fori_loop(0, panels, lambda k, c: (body(k), c)[1], 0)

    def old_panel(k):
        return old_hbm.at[0, 0, :, columns(k)]

    def old_up(k):
        return remote(old_panel(k), old_stack.at[k, rows(1)], old_send.at[k, 0], old_recv.at[k, 0], p, g + 1)

    def old_down(k):
        return remote(old_panel(k), old_stack.at[k, rows(3)], old_send.at[k, 1], old_recv.at[k, 1], p, g - 1)

    def old_back(k):
        return remote(old_panel(k), old_stack.at[k, rows(0)], old_send.at[k, 2], old_recv.at[k, 2], p - 1, g)

    def old_own(k):
        return pltpu.make_async_copy(old_panel(k), old_stack.at[k, rows(2)], own_sem.at[k])

    def halo_up(k):
        return remote(half_stack.at[k, rows(1)], half_stack.at[k, rows(0)], halo_send.at[k, 0], halo_recv.at[k, 0], p, g + 1)

    def halo_down(k):
        return remote(half_stack.at[k, rows(1)], half_stack.at[k, rows(2)], halo_send.at[k, 1], halo_recv.at[k, 1], p, g - 1)

    def step_copy():
        return remote(own_step, pair_step, step_send, step_recv, partner, g)

    def share_copy(k):
        return remote(share.at[k], pair_share.at[k], share_send.at[k], share_recv.at[k], partner, g)

    def half_chain(k):
        return remote(half_stack.at[k, rows(1)], half_in.at[k], chain_send.at[k], half_recv.at[k], p + 2, g)

    def half_relay(k):
        return remote(half_in.at[k], half_in.at[k], relay_send.at[k], half_recv.at[k], partner, g)

    def final_chain(k):
        return remote(final_out.at[k], final_in.at[k], chain_send.at[k], final_recv.at[k], p - 2, g)

    def final_relay(k):
        return remote(final_in.at[k], final_in.at[k], relay_send.at[k], final_recv.at[k], partner, g)

    def store(k):
        return pltpu.make_async_copy(final_out.at[k], out_hbm.at[0, 0, :, columns(k)], store_sem.at[k])

    loads = [
        pltpu.make_async_copy(plane_hbm.at[0, 0], plane, load_sem.at[0]),
        pltpu.make_async_copy(inverse_hbm.at[0, 0], inverse, load_sem.at[1]),
        pltpu.make_async_copy(face_hbm.at[0, 0], face, load_sem.at[2]),
        pltpu.make_async_copy(right_hbm.at[0, 0], right, load_sem.at[3]),
    ]

    barrier = pltpu.get_barrier_semaphore()
    greeted = (
        (below, p, g - 1), (above, p, g + 1), (p > 0, p - 1, g), (p < planes - 1, p + 1, g),
        (has_prev, p - 2, g), (has_next, p + 2, g),
    )
    for there, plane_to, strip_to in greeted:
        @pl.when(there)
        def _():
            pl.semaphore_signal(barrier, inc=1, device_id=(plane_to, strip_to), device_id_type=pl.DeviceIdType.MESH)
    for copy in loads:
        copy.start()
    each(lambda k: old_own(k).start())
    pl.semaphore_wait(barrier, sum(there.astype(jnp.int32) for there, _, _ in greeted))

    def send_old(k):
        pl.when(above)(lambda: old_up(k).start())
        pl.when(below)(lambda: old_down(k).start())
        pl.when(p > 0)(lambda: old_back(k).start())

    each(send_old)

    nothing = jnp.zeros((panels, size, width), jnp.bfloat16)

    @pl.when(jnp.logical_not(below))
    def _():
        old_stack[:, rows(1)] = nothing
        half_stack[:, rows(0)] = nothing

    @pl.when(jnp.logical_not(above))
    def _():
        old_stack[:, rows(3)] = nothing
        half_stack[:, rows(2)] = nothing

    @pl.when(p == planes - 1)
    def _():
        old_stack[:, rows(0)] = nothing

    @pl.when(jnp.logical_not(has_prev))
    def _():
        half_in[...] = nothing

    @pl.when(jnp.logical_not(has_next))
    def _():
        final_in[...] = nothing

    loads[0].wait()
    loads[1].wait()
    lower_step[...] = dot(inverse[...], plane[0]).astype(jnp.bfloat16)
    upper_step[...] = dot(inverse[...], plane[1]).astype(jnp.bfloat16)

    @pl.when(even)
    def _():
        own_step[...] = lower_step[...]

    @pl.when(odd == 1)
    def _():
        own_step[...] = upper_step[...]

    step_copy().start()
    loads[2].wait()
    old_weights[:, 0:size] = plane[1]
    for candidate in range(3):
        total = face[0 if candidate == 0 else 1].astype(jnp.float32) if candidate != 1 else None
        for f in (2, 3):
            named = jnp.where(links[0, 0, f] == candidate, 1.0, 0.0)
            term = face[f].astype(jnp.float32) * named
            total = term if total is None else total + term
        total = total.astype(jnp.bfloat16)
        old_weights[:, (candidate + 1) * size : (candidate + 2) * size] = total
        half_weights[:, candidate * size : (candidate + 1) * size] = total
    loads[3].wait()
    step_copy().wait()

    @pl.when(even)
    def _():
        chip_step[...] = dot(upper_step[...], pair_step[...]).astype(jnp.bfloat16)

    @pl.when(odd == 1)
    def _():
        chip_step[...] = dot(lower_step[...], pair_step[...]).astype(jnp.bfloat16)

    def prepare(k):
        old_own(k).wait()
        pl.when(p < planes - 1)(lambda: old_back(k).wait_recv())
        pl.when(below)(lambda: old_up(k).wait_recv())
        pl.when(above)(lambda: old_down(k).wait_recv())
        old_sum = right[:, columns(k)].astype(jnp.float32) - dot(old_weights[...], old_stack[k])
        value = dot(inverse[...], old_sum.astype(jnp.bfloat16))
        base[k] = value

        @pl.when(even)
        def _():
            share[k] = value.astype(jnp.bfloat16)
            share_copy(k).start()

    def send_half(k):
        pl.when(above)(lambda: halo_up(k).start())
        pl.when(below)(lambda: halo_down(k).start())

    def forward(k):
        @pl.when(odd == 1)
        def _():
            share_copy(k).wait_recv()
            before = pair_share[k]
            value = base[k] - dot(lower_step[...], before)

            @pl.when(has_prev)
            def _():
                half_chain(k).wait_recv()
                half_relay(k).start()

            arrived = half_in[k]
            half_stack[k, rows(1)] = (value + dot(chip_step[...], arrived)).astype(jnp.bfloat16)
            pl.when(has_next)(lambda: half_chain(k).start())
            send_half(k)
            prior = (before.astype(jnp.float32) - dot(pair_step[...], arrived)).astype(jnp.bfloat16)
            rest[k] = right[:, columns(k)].astype(jnp.float32) - dot(plane[0], prior)

        @pl.when(even)
        def _():
            pl.when(has_prev)(lambda: half_relay(k).wait_recv())
            arrived = half_in[k]
            half_stack[k, rows(1)] = (base[k] - dot(lower_step[...], arrived)).astype(jnp.bfloat16)
            send_half(k)
            rest[k] = right[:, columns(k)].astype(jnp.float32) - dot(plane[0], arrived)

    def turn_round(k):
        pl.when(below)(lambda: halo_up(k).wait_recv())
        pl.when(above)(lambda: halo_down(k).wait_recv())
        half_sum = rest[k] - dot(half_weights[...], half_stack[k])
        value = dot(inverse[...], half_sum.astype(jnp.bfloat16))
        base[k] = value

        @pl.when(odd == 1)
        def _():
            share[k] = value.astype(jnp.bfloat16)
            share_copy(k).start()

    def backward(k):
        @pl.when(even)
        def _():
            share_copy(k).wait_recv()
            value = base[k] - dot(upper_step[...], pair_share[k])

            @pl.when(has_next)
            def _():
                final_chain(k).wait_recv()
                final_relay(k).start()

            final_out[k] = (value + dot(chip_step[...], final_in[k])).astype(jnp.bfloat16)
            pl.when(has_prev)(lambda: final_chain(k).start())

        @pl.when(odd == 1)
        def _():
            pl.when(has_next)(lambda: final_relay(k).wait_recv())
            final_out[k] = (base[k] - dot(upper_step[...], final_in[k])).astype(jnp.bfloat16)

        store(k).start()

    to_forward = jnp.minimum(panels, LAG_FORWARD[0] + LAG_FORWARD[1] * chip)
    to_turn = to_forward + LAG_HALO
    to_backward = to_turn + jnp.minimum(panels, LAG_BACKWARD[0] + LAG_BACKWARD[1] * (chips - 1 - chip))

    def turn(t, carry):
        pl.when(t < panels)(lambda: prepare(t))
        for lag, stage in ((to_forward, forward), (to_turn, turn_round), (to_backward, backward)):
            k = t - lag
            pl.when((k >= 0) & (k < panels))(functools.partial(stage, k))
        return carry

    lax.fori_loop(0, panels + to_backward, turn, 0)

    def finish(k):
        store(k).wait()
        share_copy(k).wait_send()

        @pl.when(above)
        def _():
            old_up(k).wait_send()
            halo_up(k).wait_send()

        @pl.when(below)
        def _():
            old_down(k).wait_send()
            halo_down(k).wait_send()

        pl.when(p > 0)(lambda: old_back(k).wait_send())

        @pl.when(odd == 1)
        def _():
            pl.when(has_next)(lambda: half_chain(k).wait_send())
            pl.when(has_prev)(lambda: half_relay(k).wait_send())

        @pl.when(even)
        def _():
            pl.when(has_prev)(lambda: final_chain(k).wait_send())
            pl.when(has_next)(lambda: final_relay(k).wait_send())

    each(finish)


def local(planes, strips, right_sides, old_state, plane_coupling, face_coupling, diag_inverse, neighbours):
    size, total = right_sides.shape[2:]
    n = PANELS
    width = total // n
    half = functools.partial(pltpu.VMEM, dtype=jnp.bfloat16)
    single = functools.partial(pltpu.VMEM, dtype=jnp.float32)
    dma = pltpu.SemaphoreType.DMA
    anywhere = pl.BlockSpec(memory_space=pl.ANY)
    return pl.pallas_call(
        functools.partial(kernel, planes, strips, n),
        out_shape=jax.ShapeDtypeStruct(right_sides.shape, jnp.bfloat16),
        in_specs=[anywhere] * 5 + [pl.BlockSpec(memory_space=pltpu.SMEM)],
        out_specs=anywhere,
        scratch_shapes=[
            half((size, total)), half((2, size, size)), half((4, size, size)), half((size, size)),
            half((n, 4 * size, width)), half((n, 3 * size, width)), half((size, 4 * size)), half((size, 3 * size)),
            half((size, size)), half((size, size)), half((size, size)), half((size, size)), half((size, size)),
            single((n, size, width)), single((n, size, width)), half((n, size, width)), half((n, size, width)),
            half((n, size, width)), half((n, size, width)), half((n, size, width)),
            dma((4,)), dma((n,)), dma((n,)),
            dma((n, 3)), dma((n, 3)), dma((n, 2)), dma((n, 2)),
            dma, dma, dma((n,)), dma((n,)),
            dma((n,)), dma((n,)), dma((n,)), dma((n,)),
        ],
        compiler_params=pltpu.CompilerParams(
            collective_id=0, has_side_effects=True, vmem_limit_bytes=48 * 2**20
        ),
    )(right_sides, old_state, plane_coupling, face_coupling, diag_inverse, neighbours)


def solution(mesh):
    specs = [P("gx", "gy", *[None] * n) for n in (2, 2, 3, 3, 2, 1)]
    run = functools.partial(local, mesh.shape["gx"], mesh.shape["gy"])
    return jax.shard_map(run, mesh=mesh, in_specs=tuple(specs), out_specs=specs[0], check_vma=False)
```
